256 devices in a mesh: ta: 4 (over x), ha: 8 (over z), wa: 8 (over y, core).
Axes of the slice: x: 4, y: 4, z: 8, core: 2. Of those that a mesh axis runs over, the one named last changes fastest.
Arguments:
- latents: float32 [8, 32, 32, 384], P('ta', 'ha', 'wa'), may hold values from -6 to 6
- first_gain: float32 [384], replicated, may hold values from 0.1 to 1.9
- first_kernel: float32 [384, 3, 3, 3, 384], P('wa'), may hold values from -0.0625 to 0.0625
- first_bias: float32 [384], replicated, may hold values from -3 to 3
- second_gain: float32 [384], replicated, may hold values from 0.1 to 1.9
- second_kernel: float32 [384, 3, 3, 3, 384], P('wa'), may hold values from -0.0625 to 0.0625
- second_bias: float32 [384], replicated, may hold values from -3 to 3
- attn_gain: float32 [384], replicated, may hold values from 0.1 to 1.9
- w_query: float32 [384, 384], replicated, may hold values from -2 to 2, as said below
- w_key: float32 [384, 384], replicated, may hold values from -2 to 2, as said below
- w_value: float32 [384, 384], replicated, may hold values from -0.3125 to 0.3125
- w_out: float32 [384, 384], replicated, may hold values from -0.3125 to 0.3125
- out_bias: float32 [384], replicated, may hold values from -3 to 3
Outputs:
- decoded: float32 [8, 32, 32, 384], P('ta', 'ha', 'wa')
The draws below stay inside these ranges and needn't reach their ends.
Inputs may be any that keep to these rules, and one draw needn't show every extreme that they name: `w_query`: a dense matrix. `w_key`: a dense matrix.
All inputs are finite; a program needn't handle non-finite values.
Results may differ from the reference program's by a relative error of at most 0.00017.
Values sent between devices are 32-bit elements; how exact they have to be, the bound alone decides.
No kernel may reach another device: no remote copies, remote signals or barrier semaphores. Data moves between devices by JAX's collectives and lax.ppermute only.
A program may use at most 64 MiB of HBM per device.

```python
import math
import jax
import jax.numpy as jnp
from jax import lax

C = 384
FRAMES = 8
HEIGHT = 32
WIDTH = 32


def draw_w_query(key, part):
    return jnp.clip(jax.random.normal(jax.random.fold_in(key, 7011), (C, C), jnp.float32), -6.0, 6.0) / math.sqrt(C)


def draw_w_key(key, part):
    return jnp.clip(jax.random.normal(jax.random.fold_in(key, 7012), (C, C), jnp.float32), -6.0, 6.0) / math.sqrt(C)


def level_of(rng, shape, split, smallest, high):
    def one(axis_at, parts):
        steps = jax.random.uniform(jax.random.fold_in(jax.random.fold_in(rng, 6), axis_at), (parts,), jnp.float32, smallest / len(split), high / len(split))
        return jnp.repeat(jnp.exp(steps), shape[axis_at] // parts).reshape((-1,) + (1,) * (len(shape) - axis_at - 1))

    level = one(*split[0])
    for cut in split[1:]:
        level = level * one(*cut)
    return level


def noise(rng, shape, scale, bound, split=(), kind=jnp.bfloat16):
    values = jax.random.normal(rng, shape, jnp.float32) * scale
    if len(split) > 0:
        values = level_of(rng, shape, split, -0.22, 0.18) * values
    return jnp.clip(values, min=-bound, max=bound).astype(kind)


def setup_inputs(seed: int = 0) -> dict:
    streams_of = jax.random.split(jax.random.key(seed), 14)
    latents = noise(streams_of[0], (FRAMES, HEIGHT, WIDTH, C), 1.0, 6.0, ((0, 4), (1, 8), (2, 8)), jnp.float32)
    first_gain = jnp.clip(1.0 + 0.18 * jax.random.normal(streams_of[1], (C,), jnp.float32), 0.1, 1.9)
    first_kernel = noise(streams_of[2], (C, 3, 3, 3, C), (27 * C) ** -0.5, 0.0625, ((0, 8),), jnp.float32)
    first_bias = noise(streams_of[3], (C,), 0.5, 3.0, (), jnp.float32)
    second_gain = jnp.clip(1.0 + 0.18 * jax.random.normal(streams_of[4], (C,), jnp.float32), 0.1, 1.9)
    second_kernel = noise(streams_of[5], (C, 3, 3, 3, C), (27 * C) ** -0.5, 0.0625, ((0, 8),), jnp.float32)
    second_bias = noise(streams_of[6], (C,), 0.5, 3.0, (), jnp.float32)
    attn_gain = jnp.clip(1.0 + 0.18 * jax.random.normal(streams_of[7], (C,), jnp.float32), 0.1, 1.9)
    w_query = draw_w_query(jax.random.fold_in(streams_of[13], 71), 0)
    w_key = draw_w_key(jax.random.fold_in(streams_of[13], 71), 0)
    w_value = noise(streams_of[10], (C, C), C ** -0.5, 0.3125, (), jnp.float32)
    w_out = noise(streams_of[11], (C, C), C ** -0.5, 0.3125, (), jnp.float32)
    out_bias = noise(streams_of[12], (C,), 0.5, 3.0, (), jnp.float32)
    return dict(latents=latents, first_gain=first_gain, first_kernel=first_kernel, first_bias=first_bias, second_gain=second_gain, second_kernel=second_kernel, second_bias=second_bias, attn_gain=attn_gain, w_query=w_query, w_key=w_key, w_value=w_value, w_out=w_out, out_bias=out_bias)


def channel_norm(values, gain):
    return values * lax.rsqrt(lax.optimization_barrier(jnp.mean(values * values, axis=-1, keepdims=True)) + 1e-06) * gain

def causal_conv(values, kernel, bias):
    ordered = jnp.transpose(kernel, (1, 2, 3, 4, 0))
    result = lax.conv_general_dilated(values[None], ordered, (1, 1, 1), [(2, 0), (1, 1), (1, 1)], dimension_numbers=('NDHWC', 'DHWIO', 'NDHWC'), precision=lax.Precision.HIGHEST)
    return result[0] + bias

def reference(latents, first_gain, first_kernel, first_bias, second_gain, second_kernel, second_bias, attn_gain, w_query, w_key, w_value, w_out, out_bias):
    inner = causal_conv(jax.nn.silu(channel_norm(latents, first_gain)), first_kernel, first_bias)
    blocked = latents + causal_conv(jax.nn.silu(channel_norm(inner, second_gain)), second_kernel, second_bias)
    normed = channel_norm(blocked, attn_gain).reshape(FRAMES, HEIGHT * WIDTH, C)
    scale = 1.0 / math.sqrt(C)

    def one_frame(frame_rows):
        queries = jnp.dot(frame_rows, w_query, precision=lax.Precision.HIGHEST, preferred_element_type=jnp.float32)
        keys = jnp.dot(frame_rows, w_key, precision=lax.Precision.HIGHEST, preferred_element_type=jnp.float32)
        values = jnp.dot(frame_rows, w_value, precision=lax.Precision.HIGHEST, preferred_element_type=jnp.float32)
        scores = jnp.dot(queries, keys.T, precision=lax.Precision.HIGHEST, preferred_element_type=jnp.float32) * scale
        weights = jax.nn.softmax(scores, axis=-1)
        mixed = jnp.dot(weights, values, precision=lax.Precision.HIGHEST, preferred_element_type=jnp.float32)
        return jnp.dot(mixed, w_out, precision=lax.Precision.HIGHEST, preferred_element_type=jnp.float32)
    projected = lax.map(one_frame, normed) + out_bias
    return blocked + projected.reshape(FRAMES, HEIGHT, WIDTH, C)
```

```python
import math

import jax
import jax.numpy as jnp
from jax import lax
from jax.experimental import pallas as pl
from jax.experimental.pallas import tpu as pltpu
from jax.sharding import PartitionSpec as P

C = 384
OUT = 48
CHIPS = 4
F32 = jnp.float32
BF16 = jnp.bfloat16


Z_OFFSETS = ((0, 4), (1, -3), (2, -2), (-1, 3))


def sibling(x):
    return lax.ppermute(x, "wa", [(i, i ^ 1) for i in range(2 * CHIPS)])


def across_chips(xs):
    n = 2 * CHIPS
    return [
        lax.ppermute(x, "wa", [(i, (i + 2 * k) % n) for i in range(n)])
        for k, x in enumerate(xs, 1)
    ]


def gathered(x):
    same = [x] + across_chips([x] * (CHIPS - 1))
    return same + [sibling(piece) for piece in same]


def shifted(x, axis, by):
    n = lax.axis_size(axis)
    return lax.ppermute(x, axis, [(i, (i + by) % n) for i in range(n)])


def call(kernel, outs, *args, scratch=(), scalars=None):
    in_specs = [pl.BlockSpec(memory_space=pltpu.VMEM)] * len(args)
    if scalars is not None:
        in_specs = [pl.BlockSpec(memory_space=pltpu.SMEM)] + in_specs
        args = (scalars,) + args
    return pl.pallas_call(
        kernel,
        out_shape=[jax.ShapeDtypeStruct(s, F32) for s in outs],
        in_specs=in_specs,
        out_specs=[pl.BlockSpec(memory_space=pltpu.VMEM)] * len(outs),
        scratch_shapes=list(scratch),
        compiler_params=pltpu.CompilerParams(vmem_limit_bytes=40 * 1024 * 1024),
    )(*args)


def halves(x):
    high = x.astype(BF16)
    return high, (x - high.astype(F32)).astype(BF16)


def product(wh, wl, xh, xl):
    def dot(a, b):
        return lax.dot_general(a, b, (((1,), (0,)), ((), ())), preferred_element_type=F32)

    return dot(wh, xh) + (dot(wh, xl) + dot(wl, xh))


def activated(x, gain):
    mean = jnp.mean(x * x, axis=0, keepdims=True)
    v = x * lax.rsqrt(mean + 1e-6) * gain
    return v / (1.0 + jnp.exp(-v))


def lane_of(shape):
    return lax.broadcasted_iota(jnp.int32, shape, 1)


def columns_joined(left, mid, right):
    col = lane_of(mid.shape) & 31
    return (
        mid
        + jnp.where(col != 0, pltpu.roll(left, 1, 1), 0.0)
        + jnp.where(col != 31, pltpu.roll(right, 127, 1), 0.0)
    )


def frames_joined(first, second, third):
    late = (lane_of(second.shape) & 127) >= 64
    moved = pltpu.roll(second, 64, 1)
    own = third + jnp.where(late, moved, 0.0)
    following = first + jnp.where(late, 0.0, moved)
    return own, following


def first_conv_kernel(at, *refs):
    pieces, (gain, wh, wl) = refs[:8], refs[8:11]
    own_out, next_out, strip_out, cells, prod = refs[11:]
    y, c = at[2], at[3]
    for k in range(CHIPS):
        mine, other = pieces[k][...], pieces[CHIPS + k][...]
        both = jnp.concatenate(
            [jnp.where(c == 0, mine, other), jnp.where(c == 0, other, mine)], axis=2
        )
        chip = lax.rem(y - k + CHIPS, CHIPS)
        for f in range(2):
            for r in range(4):
                base = (r // 2) * 128 + f * 64 + (r % 2) * 32
                cells[pl.ds(pl.multiple_of(base + 8 * chip, 8), 8), :] = both[f, r]
    strip = cells[...].T
    strip_out[...] = strip
    xh, xl = halves(activated(strip, gain[...]))
    prod[...] = product(wh[...], wl[...], xh, xl)
    second_row = (lane_of((OUT, 128)) & 63) >= 32
    tiles = []
    for a in range(3):
        rows = []
        for i in range(3):
            t = 9 * a + 3 * i
            rows.append(
                [
                    columns_joined(
                        *(
                            prod[(t + j) * OUT : (t + j + 1) * OUT, p * 128 : p * 128 + 128]
                            for j in range(3)
                        )
                    )
                    for p in range(2)
                ]
            )
        down, level, up = rows
        upper = [jnp.where(second_row, pltpu.roll(v, 32, 1), 0.0) for v in level]
        lower = [jnp.where(second_row, 0.0, pltpu.roll(v, 96, 1)) for v in level]
        tiles.append(
            [
                up[0] + upper[0],
                up[1] + down[0] + lower[0] + upper[1],
                down[1] + lower[1],
            ]
        )
    for n in range(3):
        own, following = frames_joined(tiles[0][n], tiles[1][n], tiles[2][n])
        own_out[:, n * 128 : n * 128 + 128] = own
        next_out[:, n * 128 : n * 128 + 128] = following


def add_frames_kernel(at, own, arrived, top, mid, bottom):
    total = own[...] + jnp.where(at[0] > 0, arrived[...], 0.0)
    top[...] = total[:, :128]
    mid[...] = total[:, 128:256]
    bottom[...] = total[:, 256:]


def add_rows_kernel(at, top, mid, bottom, above, below, bias, out):
    h, w = at[1], 2 * at[2] + at[3]
    b = bias[pl.ds(pl.multiple_of(w * OUT, 8), OUT), :]
    second = (lane_of((OUT, 128)) & 63) >= 32
    whole_top = top[...] + above[...] + b
    whole_bottom = bottom[...] + below[...] + b
    edge_top = jnp.where(second, top[...] + b, 0.0)
    edge_bottom = jnp.where(second, 0.0, bottom[...] + b)
    out[:, :128] = jnp.where(h > 0, whole_top, edge_top)
    out[:, 128:256] = mid[...] + b
    out[:, 256:] = jnp.where(h < 7, whole_bottom, edge_bottom)


def put_channels(at, pieces, scratch):
    y, c = at[2], at[3]
    for k in range(CHIPS):
        chip = lax.rem(y - k + CHIPS, CHIPS)
        for core, piece in ((c, pieces[k]), (1 - c, pieces[CHIPS + k])):
            start = pl.multiple_of((2 * chip + core) * OUT, 8)
            scratch[pl.ds(start, OUT), :] = piece[...]


def second_conv_kernel(at, *refs):
    pieces, (gain, wh, wl) = refs[:8], refs[8:11]
    own_out, next_out, inner, prod = refs[11:]
    put_channels(at, pieces, inner)
    act = activated(inner[...], gain[...])
    top, mid, bottom = act[:, :128], act[:, 128:256], act[:, 256:]
    second_row = (lane_of((C, 128)) & 63) >= 32
    level = jnp.concatenate(
        [
            jnp.where(second_row, pltpu.roll(mid, 32, 1), pltpu.roll(top, 96, 1)),
            jnp.where(second_row, pltpu.roll(bottom, 32, 1), pltpu.roll(mid, 96, 1)),
        ],
        axis=1,
    )
    stacked = jnp.concatenate([act[:, :256], level, act[:, 128:]], axis=0)
    xh, xl = halves(stacked)
    prod[...] = product(wh[...], wl[...], xh, xl)
    for p in range(2):
        lanes = slice(p * 128, p * 128 + 128)
        joined = [
            columns_joined(
                *(prod[(3 * a + j) * OUT : (3 * a + j + 1) * OUT, lanes] for j in range(3))
            )
            for a in range(3)
        ]
        own, following = frames_joined(*joined)
        own_out[:, lanes] = own
        next_out[:, lanes] = following


def add_last_kernel(at, own, arrived, bias, out):
    w = 2 * at[2] + at[3]
    b = bias[pl.ds(pl.multiple_of(w * OUT, 8), OUT), :]
    out[...] = own[...] + jnp.where(at[0] > 0, arrived[...], 0.0) + b


def norm_kernel(at, *refs):
    pieces, (strip, gain) = refs[:8], refs[8:10]
    blocked_out, normed_out, total = refs[10:]
    put_channels(at, pieces, total)
    whole = total[...] + strip[...]
    early, late = whole[:, :128], whole[:, 128:]
    first = lane_of((C, 128)) < 64
    frame = jnp.where(
        at[3] == 0,
        jnp.where(first, early, pltpu.roll(late, 64, 1)),
        jnp.where(first, pltpu.roll(early, 64, 1), late),
    )
    blocked_out[...] = frame
    mean = jnp.mean(frame * frame, axis=0, keepdims=True)
    normed_out[...] = frame * lax.rsqrt(mean + 1e-6) * gain[...]


def query_kernel(at, blocked, normed, w_score, queries_out, rest_out, cells):
    y = at[2]
    cells[...] = blocked[...].T
    for r in range(4):
        start = pl.multiple_of(32 * r + 8 * y, 8)
        rest_out[8 * r : 8 * r + 8, :] = cells[pl.ds(start, 8), :]
    queries_out[...] = jnp.dot(
        normed[...].T, w_score[...], precision=lax.Precision.HIGHEST, preferred_element_type=F32
    )


def mix_kernel(at, queries, keys_a, keys_b, *refs):
    outs, state = refs[:CHIPS], refs[CHIPS]
    y = at[2]
    q = queries[...]
    scores = [
        jnp.dot(q, k[...], precision=lax.Precision.HIGHEST, preferred_element_type=F32)
        for k in (keys_a, keys_b)
    ]
    top = jnp.max(jnp.maximum(*scores), axis=1, keepdims=True)
    weights = [jnp.exp(s - top) for s in scores]
    denom = jnp.sum(weights[0] + weights[1], axis=1, keepdims=True)
    accum = [
        lax.dot_general(
            p,
            k[...],
            (((1,), (1,)), ((), ())),
            precision=lax.Precision.HIGHEST,
            preferred_element_type=F32,
        )
        for p, k in zip(weights, (keys_a, keys_b))
    ]
    state[:, :C] = accum[0] + accum[1]
    state[:, C:] = jnp.where(lane_of((128, 128)) < 64, top, denom)
    for k in range(CHIPS):
        chip = lax.rem(y + k, CHIPS)
        for r in range(4):
            start = pl.multiple_of(32 * r + 8 * chip, 8)
            outs[k][8 * r : 8 * r + 8, :] = state[pl.ds(start, 8), :]


def project_kernel(at, a, b, c, d, w_mixed, bias, rest, mine_out, other_out):
    parts = [x[...] for x in (a, b, c, d)]
    tops = [x[:, C : C + 1] for x in parts]
    top = jnp.maximum(jnp.maximum(tops[0], tops[1]), jnp.maximum(tops[2], tops[3]))
    factors = [jnp.exp(t - top) for t in tops]
    denom = sum(f * x[:, C + 64 : C + 65] for f, x in zip(factors, parts))
    mixed = sum(f * x[:, :C] for f, x in zip(factors, parts)) / denom
    done = rest[...] + (
        jnp.dot(mixed, w_mixed[...], precision=lax.Precision.HIGHEST, preferred_element_type=F32)
        + bias[...]
    )
    done = done.reshape(4, 8, C)
    left, right = done[:, :4], done[:, 4:]
    mine_out[...] = jnp.where(at[3] == 0, left, right)
    other_out[...] = jnp.where(at[3] == 0, right, left)


def split_weights(kernel, order):
    w = jnp.transpose(kernel, order)
    w = w.reshape(-1, math.prod(w.shape[order.index(0) + 1 :]))
    high = lax.reduce_precision(w, 8, 7)
    return high.astype(BF16), (w - high).astype(BF16)


def per_device(
    latents,
    first_gain,
    first_kernel,
    first_bias,
    second_gain,
    second_kernel,
    second_bias,
    attn_gain,
    w_query,
    w_key,
    w_value,
    w_out,
    out_bias,
):
    wa = lax.axis_index("wa")
    at = jnp.stack([lax.axis_index("ta"), lax.axis_index("ha"), wa // 2, wa % 2]).astype(jnp.int32)
    column = lambda v: v.reshape(C, 1)

    first_w = split_weights(first_kernel, (1, 2, 3, 0, 4))
    second_w = split_weights(second_kernel, (1, 3, 0, 2, 4))
    w_score = lax.dot_general(
        w_query,
        w_key,
        (((1,), (1,)), ((), ())),
        precision=lax.Precision.HIGHEST,
        preferred_element_type=F32,
    ) * (1.0 / math.sqrt(C))
    w_mixed = jnp.dot(w_value, w_out, precision=lax.Precision.HIGHEST, preferred_element_type=F32)

    own, following, strip = call(
        first_conv_kernel,
        [(OUT, 384), (OUT, 384), (C, 256)],
        *gathered(latents),
        column(first_gain),
        *first_w,
        scratch=[pltpu.VMEM((256, C), F32), pltpu.VMEM((27 * OUT, 256), F32)],
        scalars=at,
    )
    top, mid, bottom = call(
        add_frames_kernel, [(OUT, 128)] * 3, own, shifted(following, "ta", 1), scalars=at
    )
    above, below = shifted(bottom, "ha", 1), shifted(top, "ha", -1)
    (inner,) = call(
        add_rows_kernel,
        [(OUT, 384)],
        top,
        mid,
        bottom,
        above,
        below,
        column(first_bias),
        scalars=at,
    )
    own, following = call(
        second_conv_kernel,
        [(OUT, 256), (OUT, 256)],
        *gathered(inner),
        column(second_gain),
        *second_w,
        scratch=[pltpu.VMEM((C, 384), F32), pltpu.VMEM((9 * OUT, 256), F32)],
        scalars=at,
    )
    (change,) = call(
        add_last_kernel,
        [(OUT, 256)],
        own,
        shifted(following, "ta", 1),
        column(second_bias),
        scalars=at,
    )
    blocked, normed = call(
        norm_kernel,
        [(C, 128), (C, 128)],
        *gathered(change),
        strip,
        column(attn_gain),
        scratch=[pltpu.VMEM((C, 256), F32)],
        scalars=at,
    )
    keys = []
    for n in range(2):
        pairs = []
        for h in range(8):
            for w in range(8):
                offset = Z_OFFSETS[w // 2][n] * (1 if w % 2 == 0 else -1)
                pairs.append((((h + offset) % 8) * 8 + w, h * 8 + w))
        keys.append(lax.ppermute(normed, ("ha", "wa"), pairs))
    queries, rest = call(
        query_kernel,
        [(128, C), (32, C)],
        blocked,
        normed,
        w_score,
        scratch=[pltpu.VMEM((128, C), F32)],
        scalars=at,
    )
    states = call(
        mix_kernel,
        [(32, C + 128)] * CHIPS,
        queries,
        *keys,
        scratch=[pltpu.VMEM((128, C + 128), F32)],
        scalars=at,
    )
    mine, other = call(
        project_kernel,
        [(4, 4, C), (4, 4, C)],
        states[0],
        *across_chips(states[1:]),
        w_mixed,
        out_bias.reshape(1, C),
        rest,
        scalars=at,
    )
    other = sibling(other)
    even = wa % 2 == 0
    return jnp.stack([jnp.where(even, mine, other), jnp.where(even, other, mine)])


def solution(mesh):
    in_specs = (
        P("ta", "ha", "wa", None),
        P(),
        P("wa", None, None, None, None),
        P(),
        P(),
        P("wa", None, None, None, None),
        P(),
        P(),
        P(),
        P(),
        P(),
        P(),
        P(),
    )
    out_specs = P("ta", "ha", "wa", None)
    return jax.shard_map(
        per_device, mesh=mesh, in_specs=in_specs, out_specs=out_specs, check_vma=False
    )
```

```python
import math

import jax
import jax.numpy as jnp
from jax import lax
from jax.experimental import pallas as pl
from jax.experimental.pallas import tpu as pltpu
from jax.sharding import PartitionSpec as P

C = 384
OUT = 48
CHIPS = 4
F32 = jnp.float32
BF16 = jnp.bfloat16


Z_OFFSETS = ((4, 0), (-3, 1), (-2, 2), (3, -1))


def sibling(x):
    return lax.ppermute(x, "wa", [(i, i ^ 1) for i in range(2 * CHIPS)])


def across_chips(xs):
    n = 2 * CHIPS
    return [
        lax.ppermute(x, "wa", [(i, (i + 2 * k) % n) for i in range(n)])
        for k, x in enumerate(xs, 1)
    ]


def gathered(x):
    same = [x] + across_chips([x] * (CHIPS - 1))
    return same + [sibling(piece) for piece in same]


def shifted(x, axis, by):
    n = lax.axis_size(axis)
    return lax.ppermute(x, axis, [(i, (i + by) % n) for i in range(n)])


def call(kernel, outs, *args, scratch=(), scalars=None, flops=1_000_000):
    in_specs = [pl.BlockSpec(memory_space=pltpu.VMEM)] * len(args)
    outs = [o if isinstance(o, jax.ShapeDtypeStruct) else jax.ShapeDtypeStruct(o, F32) for o in outs]
    moved = sum(x.size * x.dtype.itemsize for x in (*args, *outs))
    if scalars is not None:
        in_specs = [pl.BlockSpec(memory_space=pltpu.SMEM)] + in_specs
        args = (scalars,) + args
    return pl.pallas_call(
        kernel,
        out_shape=outs,
        in_specs=in_specs,
        out_specs=[pl.BlockSpec(memory_space=pltpu.VMEM)] * len(outs),
        scratch_shapes=list(scratch),
        compiler_params=pltpu.CompilerParams(vmem_limit_bytes=40 * 1024 * 1024),
        cost_estimate=pl.CostEstimate(flops=flops, bytes_accessed=moved, transcendentals=0),
    )(*args)


def halves(x):
    high = x.astype(BF16)
    return high, (x - high.astype(F32)).astype(BF16)


def product(wh, wl, xh, xl):
    def dot(a, b):
        return lax.dot_general(a, b, (((1,), (0,)), ((), ())), preferred_element_type=F32)

    return dot(wh, xh) + (dot(wh, xl) + dot(wl, xh))


def activated(x, gain):
    mean = jnp.mean(x * x, axis=0, keepdims=True)
    v = x * lax.rsqrt(mean + 1e-6) * gain
    return v / (1.0 + jnp.exp(-v))


def lane_of(shape):
    return lax.broadcasted_iota(jnp.int32, shape, 1)


def columns_joined(left, mid, right):
    col = lane_of(mid.shape) & 31
    return (
        mid
        + jnp.where(col != 0, pltpu.roll(left, 1, 1), 0.0)
        + jnp.where(col != 31, pltpu.roll(right, 127, 1), 0.0)
    )


def frames_moved(tap):
    late = (lane_of(tap.shape) & 127) >= 64
    moved = pltpu.roll(tap, 64, 1)
    return jnp.where(late, moved, 0.0), jnp.where(late, 0.0, moved)


def one_frame(early, late, second):
    first = lane_of(early.shape) < 64
    return jnp.where(
        second,
        jnp.where(first, pltpu.roll(early, 64, 1), late),
        jnp.where(first, early, pltpu.roll(late, 64, 1)),
    )


def rows_joined(prod, a):
    second_row = (lane_of((OUT, 128)) & 63) >= 32
    rows = []
    for i in range(3):
        t = 9 * a + 3 * i
        rows.append(
            [
                columns_joined(
                    *(
                        prod[(t + j) * OUT : (t + j + 1) * OUT, p * 128 : p * 128 + 128]
                        for j in range(3)
                    )
                )
                for p in range(2)
            ]
        )
    down, level, up = rows
    upper = [jnp.where(second_row, pltpu.roll(v, 32, 1), 0.0) for v in level]
    lower = [jnp.where(second_row, 0.0, pltpu.roll(v, 96, 1)) for v in level]
    return [
        up[0] + upper[0],
        up[1] + down[0] + lower[0] + upper[1],
        down[1] + lower[1],
    ]


def first_conv_kernel(at, *refs):
    pieces, (gain, wh, wl) = refs[:8], refs[8:11]
    next_out, own_out, strip_out, xh_out, xl_out, cells, prod = refs[11:]
    y, c = at[2], at[3]
    for k in range(CHIPS):
        mine, other = pieces[k][...], pieces[CHIPS + k][...]
        both = jnp.concatenate(
            [jnp.where(c == 0, mine, other), jnp.where(c == 0, other, mine)], axis=2
        )
        chip = lax.rem(y - k + CHIPS, CHIPS)
        for f in range(2):
            for r in range(4):
                base = (r // 2) * 128 + f * 64 + (r % 2) * 32
                cells[pl.ds(pl.multiple_of(base + 8 * chip, 8), 8), :] = both[f, r]
    strip = cells[...].T
    strip_out[...] = strip
    xh, xl = halves(activated(strip, gain[...]))
    xh_out[...] = xh
    xl_out[...] = xl
    prod[...] = product(wh[...], wl[...], xh, xl)
    first, second = rows_joined(prod, 0), rows_joined(prod, 1)
    for n in range(3):
        own, following = frames_moved(second[n])
        own_out[:, n * 128 : n * 128 + 128] = own
        next_out[:, n * 128 : n * 128 + 128] = first[n] + following


def first_conv_own_kernel(xh, xl, wh, wl, earlier, own_out, prod):
    prod[...] = product(wh[...], wl[...], xh[...], xl[...])
    for n, tile in enumerate(rows_joined(prod, 0)):
        lanes = slice(n * 128, n * 128 + 128)
        own_out[:, lanes] = tile + earlier[:, lanes]


def second_conv_kernel(at, *refs):
    pieces, (gain, wh, wl) = refs[:8], refs[8:11]
    next_mine, next_other, own_mine, own_other, inner, prod = refs[11:]
    y, c = at[2], at[3]
    for k in range(CHIPS):
        chip = lax.rem(y - k + CHIPS, CHIPS)
        for core, piece in ((c, pieces[k]), (1 - c, pieces[CHIPS + k])):
            start = pl.multiple_of((2 * chip + core) * OUT, 8)
            inner[pl.ds(start, OUT), :] = piece[...]
    act = activated(inner[...], gain[...])
    top, mid, bottom = act[:, :128], act[:, 128:256], act[:, 256:]
    second_row = (lane_of((C, 128)) & 63) >= 32
    level = jnp.concatenate(
        [
            jnp.where(second_row, pltpu.roll(mid, 32, 1), pltpu.roll(top, 96, 1)),
            jnp.where(second_row, pltpu.roll(bottom, 32, 1), pltpu.roll(mid, 96, 1)),
        ],
        axis=1,
    )
    stacked = jnp.concatenate([act[:, :256], level, act[:, 128:]], axis=0)
    xh, xl = halves(stacked)
    prod[...] = product(wh[...], wl[...], xh, xl)
    following, same = [], []
    for p in range(2):
        lanes = slice(p * 128, p * 128 + 128)
        first, second, third = [
            columns_joined(
                *(prod[(3 * a + j) * OUT : (3 * a + j + 1) * OUT, lanes] for j in range(3))
            )
            for a in range(3)
        ]
        own, moved = frames_moved(second)
        same.append(third + own)
        following.append(first + moved)
    next_mine[...] = one_frame(*following, c == 1)
    next_other[...] = one_frame(*following, c == 0)
    own_mine[...] = one_frame(*same, c == 1)
    own_other[...] = one_frame(*same, c == 0)


def norm_kernel(at, *refs):
    pieces, (strip, gain) = refs[:4], refs[4:6]
    blocked_out, normed_out, total = refs[6:]
    for k in range(CHIPS):
        chip = lax.rem(at[2] - k + CHIPS, CHIPS)
        start = pl.multiple_of(chip * (2 * OUT), 8)
        total[pl.ds(start, 2 * OUT), :] = pieces[k][...]
    frame = total[...] + one_frame(strip[:, :128], strip[:, 128:], at[3] == 1)
    blocked_out[...] = frame
    mean = jnp.mean(frame * frame, axis=0, keepdims=True)
    normed_out[...] = frame * lax.rsqrt(mean + 1e-6) * gain[...]


def query_kernel(at, blocked, normed, w_score, queries_out, rest_out, cells):
    y = at[2]
    cells[...] = blocked[...].T
    for r in range(4):
        start = pl.multiple_of(32 * r + 8 * y, 8)
        rest_out[8 * r : 8 * r + 8, :] = cells[pl.ds(start, 8), :]
    queries_out[...] = jnp.dot(
        normed[...].T, w_score[...], precision=lax.Precision.HIGHEST, preferred_element_type=F32
    )


def mix_kernel(at, queries, keys_a, keys_b, *refs):
    outs, state = refs[:CHIPS], refs[CHIPS]
    q = queries[...]
    scores = [
        jnp.dot(q, k[...], precision=lax.Precision.HIGHEST, preferred_element_type=F32)
        for k in (keys_a, keys_b)
    ]
    top = jnp.max(jnp.maximum(*scores), axis=1, keepdims=True)
    weights = [jnp.exp(s - top) for s in scores]
    denom = jnp.sum(weights[0] + weights[1], axis=1, keepdims=True)
    accum = [
        lax.dot_general(
            p,
            k[...],
            (((1,), (1,)), ((), ())),
            precision=lax.Precision.HIGHEST,
            preferred_element_type=F32,
        )
        for p, k in zip(weights, (keys_a, keys_b))
    ]
    state[:, :C] = accum[0] + accum[1]
    state[:, C:] = jnp.where(lane_of((128, 128)) < 64, top, denom)
    for k in range(CHIPS):
        chip = lax.rem(at[2] + k, CHIPS)
        for r in range(4):
            start = pl.multiple_of(32 * r + 8 * chip, 8)
            outs[k][8 * r : 8 * r + 8, :] = state[pl.ds(start, 8), :]


def merged(states):
    tops = [x[:, C : C + 1] for x in states]
    top = jnp.maximum(jnp.maximum(tops[0], tops[1]), jnp.maximum(tops[2], tops[3]))
    factors = [jnp.exp(t - top) for t in tops]
    denom = sum(f * x[:, C + 64 : C + 65] for f, x in zip(factors, states))
    return sum(f * x[:, :C] for f, x in zip(factors, states)) / denom


def project_kernel(at, a, b, c, d, w_mixed, bias, rest, mine_out, other_out):
    mixed = merged([x[...] for x in (a, b, c, d)])
    done = rest[...] + (
        jnp.dot(mixed, w_mixed[...], precision=lax.Precision.HIGHEST, preferred_element_type=F32)
        + bias[...]
    )
    done = done.reshape(4, 8, C)
    left, right = done[:, :4], done[:, 4:]
    mine_out[...] = jnp.where(at[3] == 0, left, right)
    other_out[...] = jnp.where(at[3] == 0, right, left)


def split_weights(kernel, order):
    w = jnp.transpose(kernel, order)
    w = w.reshape(-1, math.prod(w.shape[order.index(0) + 1 :]))
    high = lax.reduce_precision(w, 8, 7)
    return high.astype(BF16), (w - high).astype(BF16)


def per_device(
    latents,
    first_gain,
    first_kernel,
    first_bias,
    second_gain,
    second_kernel,
    second_bias,
    attn_gain,
    w_query,
    w_key,
    w_value,
    w_out,
    out_bias,
):
    wa = lax.axis_index("wa")
    at = jnp.stack([lax.axis_index("ta"), lax.axis_index("ha"), wa // 2, wa % 2]).astype(jnp.int32)
    column = lambda v: v.reshape(C, 1)

    first_w = split_weights(first_kernel[:, :2], (1, 2, 3, 0, 4))
    first_w_own = split_weights(first_kernel[:, 2:], (1, 2, 3, 0, 4))
    second_w = split_weights(second_kernel, (1, 3, 0, 2, 4))
    w_score = lax.dot_general(
        w_query,
        w_key,
        (((1,), (1,)), ((), ())),
        precision=lax.Precision.HIGHEST,
        preferred_element_type=F32,
    ) * (1.0 / math.sqrt(C))
    w_mixed = jnp.dot(w_value, w_out, precision=lax.Precision.HIGHEST, preferred_element_type=F32)

    operand = lambda *shape: jax.ShapeDtypeStruct(shape, BF16)
    following, earlier, strip, *x = call(
        first_conv_kernel,
        [(OUT, 384), (OUT, 384), (C, 256), operand(C, 256), operand(C, 256)],
        *gathered(latents),
        column(first_gain),
        *first_w,
        scratch=[pltpu.VMEM((256, C), F32), pltpu.VMEM((18 * OUT, 256), F32)],
        scalars=at,
        flops=1_000_000_000,
    )
    arrived = shifted(following, "ta", 1)
    (own,) = call(
        first_conv_own_kernel,
        [(OUT, 384)],
        *x,
        *first_w_own,
        earlier,
        scratch=[pltpu.VMEM((9 * OUT, 256), F32)],
        flops=500_000_000,
    )
    own = own + jnp.where(at[0] > 0, arrived, 0.0)
    top, mid, bottom = own[:, :128], own[:, 128:256], own[:, 256:]
    above, below = shifted(bottom, "ha", 1), shifted(top, "ha", -1)
    second_row = (lax.broadcasted_iota(jnp.int32, (1, 128), 1) & 63) >= 32
    b = lax.dynamic_slice_in_dim(column(first_bias), wa * OUT, OUT)
    inside = jnp.where(at[1] > 0, True, second_row)
    top = jnp.where(inside, top + b + jnp.where(at[1] > 0, above, 0.0), 0.0)
    inside = jnp.where(at[1] < 7, True, ~second_row)
    bottom = jnp.where(inside, bottom + b + jnp.where(at[1] < 7, below, 0.0), 0.0)
    inner = jnp.concatenate([top, mid + b, bottom], axis=1)
    next_mine, next_other, mine, other = call(
        second_conv_kernel,
        [(OUT, 128)] * 4,
        *gathered(inner),
        column(second_gain),
        *second_w,
        scratch=[pltpu.VMEM((C, 384), F32), pltpu.VMEM((9 * OUT, 256), F32)],
        scalars=at,
        flops=1_000_000_000,
    )
    arrived = shifted(next_mine, "ta", 1)
    n = 2 * CHIPS
    arrived_other = lax.ppermute(
        next_other,
        ("ta", "wa"),
        [(t * n + i, (t + 1) % 4 * n + (i ^ 1)) for t in range(4) for i in range(n)],
    )
    mine = mine + jnp.where(at[0] > 0, arrived, 0.0)
    other = sibling(other) + jnp.where(at[0] > 0, arrived_other, 0.0)
    even = wa % 2 == 0
    change = jnp.concatenate(
        [jnp.where(even, mine, other), jnp.where(even, other, mine)], axis=0
    ) + lax.dynamic_slice_in_dim(column(second_bias), at[2] * (2 * OUT), 2 * OUT)
    blocked, normed = call(
        norm_kernel,
        [(C, 128), (C, 128)],
        change,
        *across_chips([change] * (CHIPS - 1)),
        strip,
        column(attn_gain),
        scratch=[pltpu.VMEM((C, 128), F32)],
        scalars=at,
    )
    keys = []
    for n in range(2):
        pairs = []
        for h in range(8):
            for w in range(8):
                offset = Z_OFFSETS[w // 2][n] * (1 if w % 2 == 0 else -1)
                pairs.append((((h + offset) % 8) * 8 + w, h * 8 + w))
        keys.append(lax.ppermute(normed, ("ha", "wa"), pairs))
    queries, rest = call(
        query_kernel,
        [(128, C), (32, C)],
        blocked,
        normed,
        w_score,
        scratch=[pltpu.VMEM((128, C), F32)],
        scalars=at,
    )
    states = call(
        mix_kernel,
        [(32, C + 128)] * CHIPS,
        queries,
        *keys,
        scratch=[pltpu.VMEM((128, C + 128), F32)],
        scalars=at,
    )
    mine, other = call(
        project_kernel,
        [(4, 4, C), (4, 4, C)],
        states[0],
        *across_chips(states[1:]),
        w_mixed,
        out_bias.reshape(1, C),
        rest,
        scalars=at,
    )
    other = sibling(other)
    return jnp.stack([jnp.where(even, mine, other), jnp.where(even, other, mine)])


def solution(mesh):
    in_specs = (
        P("ta", "ha", "wa", None),
        P(),
        P("wa", None, None, None, None),
        P(),
        P(),
        P("wa", None, None, None, None),
        P(),
        P(),
        P(),
        P(),
        P(),
        P(),
        P(),
    )
    out_specs = P("ta", "ha", "wa", None)
    return jax.shard_map(
        per_device, mesh=mesh, in_specs=in_specs, out_specs=out_specs, check_vma=False
    )
```

```python
import math

import jax
import jax.numpy as jnp
from jax import lax
from jax.experimental import pallas as pl
from jax.experimental.pallas import tpu as pltpu
from jax.sharding import PartitionSpec as P

C = 384
OUT = 48
CHIPS = 4
F32 = jnp.float32
BF16 = jnp.bfloat16


Z_OFFSETS = ((4, 0), (-3, 1), (-2, 2), (3, -1))


def sibling(x):
    return lax.ppermute(x, "wa", [(i, i ^ 1) for i in range(2 * CHIPS)])


def across_chips(xs):
    n = 2 * CHIPS
    return [
        lax.ppermute(x, "wa", [(i, (i + 2 * k) % n) for i in range(n)])
        for k, x in enumerate(xs, 1)
    ]


def gathered(x):
    same = [x] + across_chips([x] * (CHIPS - 1))
    return same + [sibling(piece) for piece in same]


def shifted(x, axis, by):
    n = lax.axis_size(axis)
    return lax.ppermute(x, axis, [(i, (i + by) % n) for i in range(n)])


def call(kernel, outs, *args, scratch=(), scalars=None, flops=1_000_000):
    in_specs = [pl.BlockSpec(memory_space=pltpu.VMEM)] * len(args)
    outs = [o if isinstance(o, jax.ShapeDtypeStruct) else jax.ShapeDtypeStruct(o, F32) for o in outs]
    moved = sum(x.size * x.dtype.itemsize for x in (*args, *outs))
    if scalars is not None:
        in_specs = [pl.BlockSpec(memory_space=pltpu.SMEM)] + in_specs
        args = (scalars,) + args
    return pl.pallas_call(
        kernel,
        out_shape=outs,
        in_specs=in_specs,
        out_specs=[pl.BlockSpec(memory_space=pltpu.VMEM)] * len(outs),
        scratch_shapes=list(scratch),
        compiler_params=pltpu.CompilerParams(vmem_limit_bytes=40 * 1024 * 1024),
        cost_estimate=pl.CostEstimate(flops=flops, bytes_accessed=moved, transcendentals=0),
    )(*args)


def halves(x):
    high = x.astype(BF16)
    return high, (x - high.astype(F32)).astype(BF16)


def product(wh, wl, xh, xl):
    return dot(wh, xh) + (dot(wh, xl) + dot(wl, xh))


def dot(a, b, depth=0):
    return lax.dot_general(a, b, (((1,), (depth,)), ((), ())), preferred_element_type=F32)


def thrice(x, axis, left=False):
    high, low = halves(x)
    return jnp.concatenate([high, high, low] if left else [high, low, high], axis=axis)


def activated(x, gain):
    mean = jnp.mean(x * x, axis=0, keepdims=True)
    v = x * lax.rsqrt(mean + 1e-6) * gain
    return v / (1.0 + jnp.exp(-v))


def lane_of(shape):
    return lax.broadcasted_iota(jnp.int32, shape, 1)


def columns_joined(left, mid, right):
    col = lane_of(mid.shape) & 31
    return (
        mid
        + jnp.where(col != 0, pltpu.roll(left, 1, 1), 0.0)
        + jnp.where(col != 31, pltpu.roll(right, 127, 1), 0.0)
    )


def frames_moved(tap):
    late = (lane_of(tap.shape) & 127) >= 64
    moved = pltpu.roll(tap, 64, 1)
    return jnp.where(late, moved, 0.0), jnp.where(late, 0.0, moved)


def one_frame(early, late, second):
    first = lane_of(early.shape) < 64
    return jnp.where(
        second,
        jnp.where(first, pltpu.roll(early, 64, 1), late),
        jnp.where(first, early, pltpu.roll(late, 64, 1)),
    )


def rows_joined(prod, a):
    second_row = (lane_of((OUT, 128)) & 63) >= 32
    rows = []
    for i in range(3):
        t = 9 * a + 3 * i
        rows.append(
            [
                columns_joined(
                    *(
                        prod[(t + j) * OUT : (t + j + 1) * OUT, p * 128 : p * 128 + 128]
                        for j in range(3)
                    )
                )
                for p in range(2)
            ]
        )
    down, level, up = rows
    upper = [jnp.where(second_row, pltpu.roll(v, 32, 1), 0.0) for v in level]
    lower = [jnp.where(second_row, 0.0, pltpu.roll(v, 96, 1)) for v in level]
    return [
        up[0] + upper[0],
        up[1] + down[0] + lower[0] + upper[1],
        down[1] + lower[1],
    ]


def first_conv_kernel(at, *refs):
    pieces, (gain, wh, wl) = refs[:8], refs[8:11]
    next_out, own_out, strip_out, xh_out, xl_out, cells, prod = refs[11:]
    y, c = at[2], at[3]
    for k in range(CHIPS):
        mine, other = pieces[k][...], pieces[CHIPS + k][...]
        both = jnp.concatenate(
            [jnp.where(c == 0, mine, other), jnp.where(c == 0, other, mine)], axis=2
        )
        chip = lax.rem(y - k + CHIPS, CHIPS)
        for f in range(2):
            for r in range(4):
                base = (r // 2) * 128 + f * 64 + (r % 2) * 32
                cells[pl.ds(pl.multiple_of(base + 8 * chip, 8), 8), :] = both[f, r]
    strip = cells[...].T
    strip_out[...] = strip
    xh, xl = halves(activated(strip, gain[:, 0:1]))
    xh_out[...] = xh
    xl_out[...] = xl
    prod[...] = product(wh[...], wl[...], xh, xl)
    first, second = rows_joined(prod, 0), rows_joined(prod, 1)
    for n in range(3):
        own, following = frames_moved(second[n])
        own_out[:, n * 128 : n * 128 + 128] = own
        next_out[:, n * 128 : n * 128 + 128] = first[n] + following


def first_conv_own_kernel(xh, xl, wh, wl, earlier, own_out, prod):
    prod[...] = product(wh[...], wl[...], xh[...], xl[...])
    for n, tile in enumerate(rows_joined(prod, 0)):
        lanes = slice(n * 128, n * 128 + 128)
        own_out[:, lanes] = tile + earlier[:, lanes]


def second_conv_kernel(at, *refs):
    pieces, (gain, wh, wl) = refs[:8], refs[8:11]
    next_mine, next_other, own_mine, own_other, inner, prod = refs[11:]
    y, c = at[2], at[3]
    for k in range(CHIPS):
        chip = lax.rem(y - k + CHIPS, CHIPS)
        for core, piece in ((c, pieces[k]), (1 - c, pieces[CHIPS + k])):
            start = pl.multiple_of((2 * chip + core) * OUT, 8)
            inner[pl.ds(start, OUT), :] = piece[...]
    act = activated(inner[...], gain[:, 1:2])
    top, mid, bottom = act[:, :128], act[:, 128:256], act[:, 256:]
    second_row = (lane_of((C, 128)) & 63) >= 32
    level = jnp.concatenate(
        [
            jnp.where(second_row, pltpu.roll(mid, 32, 1), pltpu.roll(top, 96, 1)),
            jnp.where(second_row, pltpu.roll(bottom, 32, 1), pltpu.roll(mid, 96, 1)),
        ],
        axis=1,
    )
    stacked = jnp.concatenate([act[:, :256], level, act[:, 128:]], axis=0)
    xh, xl = halves(stacked)
    prod[...] = product(wh[...], wl[...], xh, xl)
    following, same = [], []
    for p in range(2):
        lanes = slice(p * 128, p * 128 + 128)
        first, second, third = [
            columns_joined(
                *(prod[(3 * a + j) * OUT : (3 * a + j + 1) * OUT, lanes] for j in range(3))
            )
            for a in range(3)
        ]
        own, moved = frames_moved(second)
        same.append(third + own)
        following.append(first + moved)
    next_mine[...] = one_frame(*following, c == 1)
    next_other[...] = one_frame(*following, c == 0)
    own_mine[...] = one_frame(*same, c == 1)
    own_other[...] = one_frame(*same, c == 0)


def norm_kernel(at, *refs):
    pieces, (strip, gain) = refs[:4], refs[4:6]
    blocked_out, normed_out, total = refs[6:]
    for k in range(CHIPS):
        chip = lax.rem(at[2] - k + CHIPS, CHIPS)
        start = pl.multiple_of(chip * (2 * OUT), 8)
        total[pl.ds(start, 2 * OUT), :] = pieces[k][...]
    frame = total[...] + one_frame(strip[:, :128], strip[:, 128:], at[3] == 1)
    blocked_out[...] = frame
    mean = jnp.mean(frame * frame, axis=0, keepdims=True)
    normed_out[...] = frame * lax.rsqrt(mean + 1e-6) * gain[:, 2:3]


def query_kernel(at, blocked, normed, w_score, queries_out, rest_out, cells):
    y = at[2]
    cells[...] = blocked[...].T
    for r in range(4):
        start = pl.multiple_of(32 * r + 8 * y, 8)
        rest_out[8 * r : 8 * r + 8, :] = cells[pl.ds(start, 8), :]
    queries_out[...] = jnp.dot(
        normed[...].T, w_score[...], precision=lax.Precision.HIGHEST, preferred_element_type=F32
    )


def mix_kernel(at, queries, keys_a, keys_b, *refs):
    outs, state = refs[:CHIPS], refs[CHIPS]
    q = queries[...]
    scores = [
        jnp.dot(q, k[...], precision=lax.Precision.HIGHEST, preferred_element_type=F32)
        for k in (keys_a, keys_b)
    ]
    top = jnp.max(jnp.maximum(*scores), axis=1, keepdims=True)
    weights = [jnp.exp(s - top) for s in scores]
    denom = jnp.sum(weights[0] + weights[1], axis=1, keepdims=True)
    state[:, :C] = dot(
        jnp.concatenate([thrice(p, 1, left=True) for p in weights], axis=1),
        jnp.concatenate([thrice(k[...], 1) for k in (keys_a, keys_b)], axis=1),
        depth=1,
    )
    state[:, C:] = jnp.where(lane_of((128, 128)) < 64, top, denom)
    for k in range(CHIPS):
        chip = lax.rem(at[2] + k, CHIPS)
        for r in range(4):
            start = pl.multiple_of(32 * r + 8 * chip, 8)
            outs[k][8 * r : 8 * r + 8, :] = state[pl.ds(start, 8), :]


def merged(states):
    tops = [x[:, C : C + 1] for x in states]
    top = jnp.maximum(jnp.maximum(tops[0], tops[1]), jnp.maximum(tops[2], tops[3]))
    factors = [jnp.exp(t - top) for t in tops]
    denom = sum(f * x[:, C + 64 : C + 65] for f, x in zip(factors, states))
    return sum(f * x[:, :C] for f, x in zip(factors, states)) / denom


def project_kernel(at, a, b, c, d, w_mixed, bias, rest, mine_out, other_out):
    mixed = merged([x[...] for x in (a, b, c, d)])
    projected = dot(thrice(mixed, 1, left=True), thrice(w_mixed[...], 0))
    done = rest[...] + (projected + bias[...])
    done = done.reshape(4, 8, C)
    left, right = done[:, :4], done[:, 4:]
    mine_out[...] = jnp.where(at[3] == 0, left, right)
    other_out[...] = jnp.where(at[3] == 0, right, left)


def split_weights(kernel, order):
    w = jnp.transpose(kernel, order)
    w = w.reshape(-1, math.prod(w.shape[order.index(0) + 1 :]))
    high = lax.reduce_precision(w, 8, 7)
    return high.astype(BF16), (w - high).astype(BF16)


def per_device(
    latents,
    first_gain,
    first_kernel,
    first_bias,
    second_gain,
    second_kernel,
    second_bias,
    attn_gain,
    w_query,
    w_key,
    w_value,
    w_out,
    out_bias,
):
    wa = lax.axis_index("wa")
    at = jnp.stack([lax.axis_index("ta"), lax.axis_index("ha"), wa // 2, wa % 2]).astype(jnp.int32)
    column = lambda v: v.reshape(C, 1)
    gains = jnp.stack([first_gain, second_gain, attn_gain], axis=1)

    first_w = split_weights(first_kernel[:, :2], (1, 2, 3, 0, 4))
    first_w_own = split_weights(first_kernel[:, 2:], (1, 2, 3, 0, 4))
    second_w = split_weights(second_kernel, (1, 3, 0, 2, 4))
    w_score = lax.dot_general(
        w_query,
        w_key,
        (((1,), (1,)), ((), ())),
        precision=lax.Precision.HIGHEST,
        preferred_element_type=F32,
    ) * (1.0 / math.sqrt(C))
    w_mixed = jnp.dot(w_value, w_out, precision=lax.Precision.HIGHEST, preferred_element_type=F32)

    operand = lambda *shape: jax.ShapeDtypeStruct(shape, BF16)
    following, earlier, strip, *x = call(
        first_conv_kernel,
        [(OUT, 384), (OUT, 384), (C, 256), operand(C, 256), operand(C, 256)],
        *gathered(latents),
        gains,
        *first_w,
        scratch=[pltpu.VMEM((256, C), F32), pltpu.VMEM((18 * OUT, 256), F32)],
        scalars=at,
        flops=1_000_000_000,
    )
    arrived = shifted(following, "ta", 1)
    (own,) = call(
        first_conv_own_kernel,
        [(OUT, 384)],
        *x,
        *first_w_own,
        earlier,
        scratch=[pltpu.VMEM((9 * OUT, 256), F32)],
        flops=500_000_000,
    )
    own = own + jnp.where(at[0] > 0, arrived, 0.0)
    top, mid, bottom = own[:, :128], own[:, 128:256], own[:, 256:]
    above, below = shifted(bottom, "ha", 1), shifted(top, "ha", -1)
    second_row = (lax.broadcasted_iota(jnp.int32, (1, 128), 1) & 63) >= 32
    b = lax.dynamic_slice_in_dim(column(first_bias), wa * OUT, OUT)
    inside = jnp.where(at[1] > 0, True, second_row)
    top = jnp.where(inside, top + b + jnp.where(at[1] > 0, above, 0.0), 0.0)
    inside = jnp.where(at[1] < 7, True, ~second_row)
    bottom = jnp.where(inside, bottom + b + jnp.where(at[1] < 7, below, 0.0), 0.0)
    inner = jnp.concatenate([top, mid + b, bottom], axis=1)
    next_mine, next_other, mine, other = call(
        second_conv_kernel,
        [(OUT, 128)] * 4,
        *gathered(inner),
        gains,
        *second_w,
        scratch=[pltpu.VMEM((C, 384), F32), pltpu.VMEM((9 * OUT, 256), F32)],
        scalars=at,
        flops=1_000_000_000,
    )
    arrived = shifted(next_mine, "ta", 1)
    n = 2 * CHIPS
    arrived_other = lax.ppermute(
        next_other,
        ("ta", "wa"),
        [(t * n + i, (t + 1) % 4 * n + (i ^ 1)) for t in range(4) for i in range(n)],
    )
    mine = mine + jnp.where(at[0] > 0, arrived, 0.0)
    other = sibling(other) + jnp.where(at[0] > 0, arrived_other, 0.0)
    even = wa % 2 == 0
    change = jnp.concatenate(
        [jnp.where(even, mine, other), jnp.where(even, other, mine)], axis=0
    ) + lax.dynamic_slice_in_dim(column(second_bias), at[2] * (2 * OUT), 2 * OUT)
    blocked, normed = call(
        norm_kernel,
        [(C, 128), (C, 128)],
        change,
        *across_chips([change] * (CHIPS - 1)),
        strip,
        gains,
        scratch=[pltpu.VMEM((C, 128), F32)],
        scalars=at,
    )
    keys = []
    for n in range(2):
        pairs = []
        for h in range(8):
            for w in range(8):
                offset = Z_OFFSETS[w // 2][n] * (1 if w % 2 == 0 else -1)
                pairs.append((((h + offset) % 8) * 8 + w, h * 8 + w))
        keys.append(lax.ppermute(normed, ("ha", "wa"), pairs))
    queries, rest = call(
        query_kernel,
        [(128, C), (32, C)],
        blocked,
        normed,
        w_score,
        scratch=[pltpu.VMEM((128, C), F32)],
        scalars=at,
    )
    states = call(
        mix_kernel,
        [(32, C + 128)] * CHIPS,
        queries,
        *keys,
        scratch=[pltpu.VMEM((128, C + 128), F32)],
        scalars=at,
    )
    mine, other = call(
        project_kernel,
        [(4, 4, C), (4, 4, C)],
        states[0],
        *across_chips(states[1:]),
        w_mixed,
        out_bias.reshape(1, C),
        rest,
        scalars=at,
    )
    other = sibling(other)
    return jnp.stack([jnp.where(even, mine, other), jnp.where(even, other, mine)])


def solution(mesh):
    in_specs = (
        P("ta", "ha", "wa", None),
        P(),
        P("wa", None, None, None, None),
        P(),
        P(),
        P("wa", None, None, None, None),
        P(),
        P(),
        P(),
        P(),
        P(),
        P(),
        P(),
    )
    out_specs = P("ta", "ha", "wa", None)
    return jax.shard_map(
        per_device, mesh=mesh, in_specs=in_specs, out_specs=out_specs, check_vma=False
    )
```

```python
import math

import jax
import jax.numpy as jnp
from jax import lax
from jax.experimental import pallas as pl
from jax.experimental.pallas import tpu as pltpu
from jax.sharding import PartitionSpec as P

C = 384
OUT = 48
CHIPS = 4
F32 = jnp.float32
BF16 = jnp.bfloat16


Z_OFFSETS = ((4, 0), (-3, 1), (-2, 2), (3, -1))


def sibling(x):
    return lax.ppermute(x, "wa", [(i, i ^ 1) for i in range(2 * CHIPS)])


def across_chips(xs):
    n = 2 * CHIPS
    return [
        lax.ppermute(x, "wa", [(i, (i + 2 * k * (1 - 2 * (i % 2))) % n) for i in range(n)])
        for k, x in enumerate(xs, 1)
    ]


def chip_away(at, k):
    return lax.rem(at[2] + (1 - 2 * at[3]) * k + CHIPS, CHIPS)


def gathered(x):
    same = [x] + across_chips([x] * (CHIPS - 1))
    return same + [sibling(piece) for piece in same]


def shifted(x, axis, by):
    n = lax.axis_size(axis)
    return lax.ppermute(x, axis, [(i, (i + by) % n) for i in range(n)])


def call(kernel, outs, *args, scratch=(), scalars=None, flops=1_000_000):
    in_specs = [pl.BlockSpec(memory_space=pltpu.VMEM)] * len(args)
    outs = [o if isinstance(o, jax.ShapeDtypeStruct) else jax.ShapeDtypeStruct(o, F32) for o in outs]
    moved = sum(x.size * x.dtype.itemsize for x in (*args, *outs))
    if scalars is not None:
        in_specs = [pl.BlockSpec(memory_space=pltpu.SMEM)] + in_specs
        args = (scalars,) + args
    return pl.pallas_call(
        kernel,
        out_shape=outs,
        in_specs=in_specs,
        out_specs=[pl.BlockSpec(memory_space=pltpu.VMEM)] * len(outs),
        scratch_shapes=list(scratch),
        compiler_params=pltpu.CompilerParams(vmem_limit_bytes=40 * 1024 * 1024),
        cost_estimate=pl.CostEstimate(flops=flops, bytes_accessed=moved, transcendentals=0),
    )(*args)


def halves(x):
    high = x.astype(BF16)
    return high, (x - high.astype(F32)).astype(BF16)


def product(wh, wl, xh, xl):
    return dot(wh, xh) + (dot(wh, xl) + dot(wl, xh))


def dot(a, b, depth=0):
    return lax.dot_general(a, b, (((1,), (depth,)), ((), ())), preferred_element_type=F32)


def thrice(x, axis, left=False):
    high, low = halves(x)
    return jnp.concatenate([high, high, low] if left else [high, low, high], axis=axis)


def activated(x, gain):
    mean = jnp.mean(x * x, axis=0, keepdims=True)
    v = x * lax.rsqrt(mean + 1e-6) * gain
    return v / (1.0 + jnp.exp(-v))


def lane_of(shape):
    return lax.broadcasted_iota(jnp.int32, shape, 1)


def columns_joined(left, mid, right):
    col = lane_of(mid.shape) & 31
    return (
        mid
        + jnp.where(col != 0, pltpu.roll(left, 1, 1), 0.0)
        + jnp.where(col != 31, pltpu.roll(right, 127, 1), 0.0)
    )


def frames_moved(tap):
    late = (lane_of(tap.shape) & 127) >= 64
    moved = pltpu.roll(tap, 64, 1)
    return jnp.where(late, moved, 0.0), jnp.where(late, 0.0, moved)


def one_frame(early, late, second):
    first = lane_of(early.shape) < 64
    return jnp.where(
        second,
        jnp.where(first, pltpu.roll(early, 64, 1), late),
        jnp.where(first, early, pltpu.roll(late, 64, 1)),
    )


def rows_joined(prod, a):
    second_row = (lane_of((OUT, 128)) & 63) >= 32
    rows = []
    for i in range(3):
        t = 9 * a + 3 * i
        rows.append(
            [
                columns_joined(
                    *(
                        prod[(t + j) * OUT : (t + j + 1) * OUT, p * 128 : p * 128 + 128]
                        for j in range(3)
                    )
                )
                for p in range(2)
            ]
        )
    down, level, up = rows
    upper = [jnp.where(second_row, pltpu.roll(v, 32, 1), 0.0) for v in level]
    lower = [jnp.where(second_row, 0.0, pltpu.roll(v, 96, 1)) for v in level]
    return [
        up[0] + upper[0],
        up[1] + down[0] + lower[0] + upper[1],
        down[1] + lower[1],
    ]


def first_conv_kernel(at, *refs):
    pieces, (gain, wh, wl) = refs[:8], refs[8:11]
    next_out, own_out, strip_out, xh_out, xl_out, cells, prod = refs[11:]
    c = at[3]
    for k in range(CHIPS):
        mine, other = pieces[k][...], pieces[CHIPS + (CHIPS - k) % CHIPS][...]
        both = jnp.concatenate(
            [jnp.where(c == 0, mine, other), jnp.where(c == 0, other, mine)], axis=2
        )
        chip = chip_away(at, -k)
        for f in range(2):
            for r in range(4):
                base = (r // 2) * 128 + f * 64 + (r % 2) * 32
                cells[pl.ds(pl.multiple_of(base + 8 * chip, 8), 8), :] = both[f, r]
    strip = cells[...].T
    strip_out[...] = strip
    xh, xl = halves(activated(strip, gain[...]))
    xh_out[...] = xh
    xl_out[...] = xl
    prod[...] = product(wh[...], wl[...], xh, xl)
    first, second = rows_joined(prod, 0), rows_joined(prod, 1)
    for n in range(3):
        own, following = frames_moved(second[n])
        own_out[:, n * 128 : n * 128 + 128] = own
        next_out[:, n * 128 : n * 128 + 128] = first[n] + following


def first_conv_own_kernel(xh, xl, wh, wl, earlier, own_out, prod):
    prod[...] = product(wh[...], wl[...], xh[...], xl[...])
    for n, tile in enumerate(rows_joined(prod, 0)):
        lanes = slice(n * 128, n * 128 + 128)
        own_out[:, lanes] = tile + earlier[:, lanes]


def second_conv_kernel(at, *refs):
    pieces, (gain, wh, wl) = refs[:8], refs[8:11]
    next_mine, next_other, own_mine, own_other, inner, prod = refs[11:]
    c = at[3]
    for k in range(CHIPS):
        chip = chip_away(at, -k)
        for core, piece in ((c, pieces[k]), (1 - c, pieces[CHIPS + (CHIPS - k) % CHIPS])):
            start = pl.multiple_of((2 * chip + core) * OUT, 8)
            inner[pl.ds(start, OUT), :] = piece[...]
    act = activated(inner[...], gain[...])
    top, mid, bottom = act[:, :128], act[:, 128:256], act[:, 256:]
    second_row = (lane_of((C, 128)) & 63) >= 32
    level = jnp.concatenate(
        [
            jnp.where(second_row, pltpu.roll(mid, 32, 1), pltpu.roll(top, 96, 1)),
            jnp.where(second_row, pltpu.roll(bottom, 32, 1), pltpu.roll(mid, 96, 1)),
        ],
        axis=1,
    )
    stacked = jnp.concatenate([act[:, :256], level, act[:, 128:]], axis=0)
    xh, xl = halves(stacked)
    prod[...] = product(wh[...], wl[...], xh, xl)
    following, same = [], []
    for p in range(2):
        lanes = slice(p * 128, p * 128 + 128)
        first, second, third = [
            columns_joined(
                *(prod[(3 * a + j) * OUT : (3 * a + j + 1) * OUT, lanes] for j in range(3))
            )
            for a in range(3)
        ]
        own, moved = frames_moved(second)
        same.append(third + own)
        following.append(first + moved)
    next_mine[...] = one_frame(*following, c == 1)
    next_other[...] = one_frame(*following, c == 0)
    own_mine[...] = one_frame(*same, c == 1)
    own_other[...] = one_frame(*same, c == 0)


def norm_kernel(at, *refs):
    pieces, (strip, gain) = refs[:4], refs[4:6]
    blocked_out, normed_out, total = refs[6:]
    for k in range(CHIPS):
        chip = chip_away(at, -k)
        start = pl.multiple_of(chip * (2 * OUT), 8)
        total[pl.ds(start, 2 * OUT), :] = pieces[k][...]
    frame = total[...] + one_frame(strip[:, :128], strip[:, 128:], at[3] == 1)
    blocked_out[...] = frame
    mean = jnp.mean(frame * frame, axis=0, keepdims=True)
    normed_out[...] = frame * lax.rsqrt(mean + 1e-6) * gain[...]


def query_kernel(at, blocked, normed, w_score, queries_out, rest_out, cells):
    y = at[2]
    cells[...] = blocked[...].T
    for r in range(4):
        start = pl.multiple_of(32 * r + 8 * y, 8)
        rest_out[8 * r : 8 * r + 8, :] = cells[pl.ds(start, 8), :]
    queries_out[...] = jnp.dot(
        normed[...].T, w_score[...], precision=lax.Precision.HIGHEST, preferred_element_type=F32
    )


def mix_kernel(at, queries, keys_a, keys_b, *refs):
    outs, state = refs[:CHIPS], refs[CHIPS]
    q = queries[...]
    scores = [
        jnp.dot(q, k[...], precision=lax.Precision.HIGHEST, preferred_element_type=F32)
        for k in (keys_a, keys_b)
    ]
    top = jnp.max(jnp.maximum(*scores), axis=1, keepdims=True)
    weights = [jnp.exp(s - top) for s in scores]
    denom = jnp.sum(weights[0] + weights[1], axis=1, keepdims=True)
    state[:, :C] = dot(
        jnp.concatenate([thrice(p, 1, left=True) for p in weights], axis=1),
        jnp.concatenate([thrice(k[...], 1) for k in (keys_a, keys_b)], axis=1),
        depth=1,
    )
    state[:, C:] = jnp.where(lane_of((128, 128)) < 64, top, denom)
    for k in range(CHIPS):
        chip = chip_away(at, k)
        for r in range(4):
            start = pl.multiple_of(32 * r + 8 * chip, 8)
            outs[k][8 * r : 8 * r + 8, :] = state[pl.ds(start, 8), :]


def merged(states):
    tops = [x[:, C : C + 1] for x in states]
    top = jnp.maximum(jnp.maximum(tops[0], tops[1]), jnp.maximum(tops[2], tops[3]))
    factors = [jnp.exp(t - top) for t in tops]
    denom = sum(f * x[:, C + 64 : C + 65] for f, x in zip(factors, states))
    return sum(f * x[:, :C] for f, x in zip(factors, states)) / denom


def project_kernel(at, a, b, c, d, w_mixed, bias, rest, mine_out, other_out):
    mixed = merged([x[...] for x in (a, b, c, d)])
    projected = dot(thrice(mixed, 1, left=True), thrice(w_mixed[...], 0))
    done = rest[...] + (projected + bias[...])
    done = done.reshape(4, 8, C)
    left, right = done[:, :4], done[:, 4:]
    mine_out[...] = jnp.where(at[3] == 0, left, right)
    other_out[...] = jnp.where(at[3] == 0, right, left)


def split_weights(kernel, order):
    w = jnp.transpose(kernel, order)
    w = w.reshape(-1, math.prod(w.shape[order.index(0) + 1 :]))
    high = lax.reduce_precision(w, 8, 7)
    return high.astype(BF16), (w - high).astype(BF16)


def per_device(
    latents,
    first_gain,
    first_kernel,
    first_bias,
    second_gain,
    second_kernel,
    second_bias,
    attn_gain,
    w_query,
    w_key,
    w_value,
    w_out,
    out_bias,
):
    wa = lax.axis_index("wa")
    at = jnp.stack([lax.axis_index("ta"), lax.axis_index("ha"), wa // 2, wa % 2]).astype(jnp.int32)
    column = lambda v: v.reshape(C, 1)

    first_w = split_weights(first_kernel[:, :2], (1, 2, 3, 0, 4))
    first_w_own = split_weights(first_kernel[:, 2:], (1, 2, 3, 0, 4))
    second_w = split_weights(second_kernel, (1, 3, 0, 2, 4))
    w_score = lax.dot_general(
        w_query,
        w_key,
        (((1,), (1,)), ((), ())),
        precision=lax.Precision.HIGHEST,
        preferred_element_type=F32,
    ) * (1.0 / math.sqrt(C))
    w_mixed = jnp.dot(w_value, w_out, precision=lax.Precision.HIGHEST, preferred_element_type=F32)

    operand = lambda *shape: jax.ShapeDtypeStruct(shape, BF16)
    following, earlier, strip, *x = call(
        first_conv_kernel,
        [(OUT, 384), (OUT, 384), (C, 256), operand(C, 256), operand(C, 256)],
        *gathered(latents),
        column(first_gain),
        *first_w,
        scratch=[pltpu.VMEM((256, C), F32), pltpu.VMEM((18 * OUT, 256), F32)],
        scalars=at,
        flops=1_000_000_000,
    )
    arrived = shifted(following, "ta", 1)
    (own,) = call(
        first_conv_own_kernel,
        [(OUT, 384)],
        *x,
        *first_w_own,
        earlier,
        scratch=[pltpu.VMEM((9 * OUT, 256), F32)],
        flops=500_000_000,
    )
    own = own + jnp.where(at[0] > 0, arrived, 0.0)
    top, mid, bottom = own[:, :128], own[:, 128:256], own[:, 256:]
    above, below = shifted(bottom, "ha", 1), shifted(top, "ha", -1)
    second_row = (lax.broadcasted_iota(jnp.int32, (1, 128), 1) & 63) >= 32
    b = lax.dynamic_slice_in_dim(column(first_bias), wa * OUT, OUT)
    inside = jnp.where(at[1] > 0, True, second_row)
    top = jnp.where(inside, top + b + jnp.where(at[1] > 0, above, 0.0), 0.0)
    inside = jnp.where(at[1] < 7, True, ~second_row)
    bottom = jnp.where(inside, bottom + b + jnp.where(at[1] < 7, below, 0.0), 0.0)
    inner = jnp.concatenate([top, mid + b, bottom], axis=1)
    next_mine, next_other, mine, other = call(
        second_conv_kernel,
        [(OUT, 128)] * 4,
        *gathered(inner),
        column(second_gain),
        *second_w,
        scratch=[pltpu.VMEM((C, 384), F32), pltpu.VMEM((9 * OUT, 256), F32)],
        scalars=at,
        flops=1_000_000_000,
    )
    arrived = shifted(next_mine, "ta", 1)
    n = 2 * CHIPS
    arrived_other = lax.ppermute(
        next_other,
        ("ta", "wa"),
        [(t * n + i, (t + 1) % 4 * n + (i ^ 1)) for t in range(4) for i in range(n)],
    )
    mine = mine + jnp.where(at[0] > 0, arrived, 0.0)
    other = sibling(other) + jnp.where(at[0] > 0, arrived_other, 0.0)
    even = wa % 2 == 0
    change = jnp.concatenate(
        [jnp.where(even, mine, other), jnp.where(even, other, mine)], axis=0
    ) + lax.dynamic_slice_in_dim(column(second_bias), at[2] * (2 * OUT), 2 * OUT)
    blocked, normed = call(
        norm_kernel,
        [(C, 128), (C, 128)],
        change,
        *across_chips([change] * (CHIPS - 1)),
        strip,
        column(attn_gain),
        scratch=[pltpu.VMEM((C, 128), F32)],
        scalars=at,
    )
    keys = []
    for n in range(2):
        pairs = []
        for h in range(8):
            for w in range(8):
                offset = Z_OFFSETS[w // 2][n] * (1 if w % 2 == 0 else -1)
                pairs.append((((h + offset) % 8) * 8 + w, h * 8 + w))
        keys.append(lax.ppermute(normed, ("ha", "wa"), pairs))
    queries, rest = call(
        query_kernel,
        [(128, C), (32, C)],
        blocked,
        normed,
        w_score,
        scratch=[pltpu.VMEM((128, C), F32)],
        scalars=at,
    )
    states = call(
        mix_kernel,
        [(32, C + 128)] * CHIPS,
        queries,
        *keys,
        scratch=[pltpu.VMEM((128, C + 128), F32)],
        scalars=at,
    )
    mine, other = call(
        project_kernel,
        [(4, 4, C), (4, 4, C)],
        states[0],
        *across_chips(states[1:]),
        w_mixed,
        out_bias.reshape(1, C),
        rest,
        scalars=at,
    )
    other = sibling(other)
    return jnp.stack([jnp.where(even, mine, other), jnp.where(even, other, mine)])


def solution(mesh):
    in_specs = (
        P("ta", "ha", "wa", None),
        P(),
        P("wa", None, None, None, None),
        P(),
        P(),
        P("wa", None, None, None, None),
        P(),
        P(),
        P(),
        P(),
        P(),
        P(),
        P(),
    )
    out_specs = P("ta", "ha", "wa", None)
    return jax.shard_map(
        per_device, mesh=mesh, in_specs=in_specs, out_specs=out_specs, check_vma=False
    )
```

```python
import math

import jax
import jax.numpy as jnp
from jax import lax
from jax.experimental import pallas as pl
from jax.experimental.pallas import tpu as pltpu
from jax.sharding import PartitionSpec as P

C = 384
OUT = 48
CHIPS = 4
F32 = jnp.float32
BF16 = jnp.bfloat16


Z_OFFSETS = ((4, 0), (-3, 1), (-2, 2), (3, -1))


def sibling(x):
    return lax.ppermute(x, "wa", [(i, i ^ 1) for i in range(2 * CHIPS)])


def across_chips(xs):
    n = 2 * CHIPS
    return [
        lax.ppermute(x, "wa", [(i, (i + 2 * k * (1 - 2 * (i % 2))) % n) for i in range(n)])
        for k, x in enumerate(xs, 1)
    ]


def chip_away(at, k):
    return lax.rem(at[2] + (1 - 2 * at[3]) * k + CHIPS, CHIPS)


def gathered(x):
    same = [x] + across_chips([x] * (CHIPS - 1))
    return same + [sibling(piece) for piece in same]


def shifted(x, axis, by):
    n = lax.axis_size(axis)
    return lax.ppermute(x, axis, [(i, (i + by) % n) for i in range(n)])


def call(kernel, outs, *args, scratch=(), scalars=None, flops=1_000_000):
    in_specs = [pl.BlockSpec(memory_space=pltpu.VMEM)] * len(args)
    outs = [o if isinstance(o, jax.ShapeDtypeStruct) else jax.ShapeDtypeStruct(o, F32) for o in outs]
    moved = sum(x.size * x.dtype.itemsize for x in (*args, *outs))
    if scalars is not None:
        in_specs = [pl.BlockSpec(memory_space=pltpu.SMEM)] + in_specs
        args = (scalars,) + args
    return pl.pallas_call(
        kernel,
        out_shape=outs,
        in_specs=in_specs,
        out_specs=[pl.BlockSpec(memory_space=pltpu.VMEM)] * len(outs),
        scratch_shapes=list(scratch),
        compiler_params=pltpu.CompilerParams(vmem_limit_bytes=40 * 1024 * 1024),
        cost_estimate=pl.CostEstimate(flops=flops, bytes_accessed=moved, transcendentals=0),
    )(*args)


def halves(x):
    high = x.astype(BF16)
    return high, (x - high.astype(F32)).astype(BF16)


def product(wh, wl, xh, xl):
    return dot(wh, xh) + (dot(wh, xl) + dot(wl, xh))


def dot(a, b, depth=0):
    return lax.dot_general(a, b, (((1,), (depth,)), ((), ())), preferred_element_type=F32)


def thrice(x, axis, left=False):
    high, low = halves(x)
    return jnp.concatenate([high, high, low] if left else [high, low, high], axis=axis)


def activated(x, gain):
    mean = jnp.mean(x * x, axis=0, keepdims=True)
    v = x * lax.rsqrt(mean + 1e-6) * gain
    return v / (1.0 + jnp.exp(-v))


def lane_of(shape):
    return lax.broadcasted_iota(jnp.int32, shape, 1)


def columns_joined(left, mid, right):
    col = lane_of(mid.shape) & 31
    return (
        mid
        + jnp.where(col != 0, pltpu.roll(left, 1, 1), 0.0)
        + jnp.where(col != 31, pltpu.roll(right, 127, 1), 0.0)
    )


def frames_moved(tap):
    late = (lane_of(tap.shape) & 127) >= 64
    moved = pltpu.roll(tap, 64, 1)
    return jnp.where(late, moved, 0.0), jnp.where(late, 0.0, moved)


def one_frame(early, late, second):
    first = lane_of(early.shape) < 64
    return jnp.where(
        second,
        jnp.where(first, pltpu.roll(early, 64, 1), late),
        jnp.where(first, early, pltpu.roll(late, 64, 1)),
    )


def rows_joined(prod, a):
    second_row = (lane_of((OUT, 128)) & 63) >= 32
    rows = []
    for i in range(3):
        t = 9 * a + 3 * i
        rows.append(
            [
                columns_joined(
                    *(
                        prod[(t + j) * OUT : (t + j + 1) * OUT, p * 128 : p * 128 + 128]
                        for j in range(3)
                    )
                )
                for p in range(2)
            ]
        )
    down, level, up = rows
    upper = [jnp.where(second_row, pltpu.roll(v, 32, 1), 0.0) for v in level]
    lower = [jnp.where(second_row, 0.0, pltpu.roll(v, 96, 1)) for v in level]
    return [
        up[0] + upper[0],
        up[1] + down[0] + lower[0] + upper[1],
        down[1] + lower[1],
    ]


def first_conv_kernel(at, *refs):
    pieces, (gain, wh, wl) = refs[:8], refs[8:11]
    next_out, own_out, strip_out, xh_out, xl_out, cells, prod = refs[11:]
    c = at[3]
    for k in range(CHIPS):
        mine, other = pieces[k][...], pieces[CHIPS + (CHIPS - k) % CHIPS][...]
        both = jnp.concatenate(
            [jnp.where(c == 0, mine, other), jnp.where(c == 0, other, mine)], axis=2
        )
        chip = chip_away(at, -k)
        for f in range(2):
            for r in range(4):
                base = (r // 2) * 128 + f * 64 + (r % 2) * 32
                cells[pl.ds(pl.multiple_of(base + 8 * chip, 8), 8), :] = both[f, r]
    strip = cells[...].T
    strip_out[...] = strip
    xh, xl = halves(activated(strip, gain[...]))
    xh_out[...] = xh
    xl_out[...] = xl
    prod[...] = product(wh[...], wl[...], xh, xl)
    first, second = rows_joined(prod, 0), rows_joined(prod, 1)
    for n in range(3):
        own, following = frames_moved(second[n])
        own_out[:, n * 128 : n * 128 + 128] = own
        next_out[:, n * 128 : n * 128 + 128] = first[n] + following


def first_conv_own_kernel(at, xh, xl, wh, wl, earlier, strip, own_out, frame_out, prod):
    frame_out[...] = one_frame(strip[:, :128], strip[:, 128:], at[3] == 1)
    prod[...] = product(wh[...], wl[...], xh[...], xl[...])
    for n, tile in enumerate(rows_joined(prod, 0)):
        lanes = slice(n * 128, n * 128 + 128)
        own_out[:, lanes] = tile + earlier[:, lanes]


def second_conv_kernel(at, *refs):
    pieces, (gain, wh, wl) = refs[:8], refs[8:11]
    next_mine, next_other, own_mine, own_other, inner, prod = refs[11:]
    c = at[3]
    for k in range(CHIPS):
        chip = chip_away(at, -k)
        for core, piece in ((c, pieces[k]), (1 - c, pieces[CHIPS + (CHIPS - k) % CHIPS])):
            start = pl.multiple_of((2 * chip + core) * OUT, 8)
            inner[pl.ds(start, OUT), :] = piece[...]
    act = activated(inner[...], gain[...])
    top, mid, bottom = act[:, :128], act[:, 128:256], act[:, 256:]
    second_row = (lane_of((C, 128)) & 63) >= 32
    level = jnp.concatenate(
        [
            jnp.where(second_row, pltpu.roll(mid, 32, 1), pltpu.roll(top, 96, 1)),
            jnp.where(second_row, pltpu.roll(bottom, 32, 1), pltpu.roll(mid, 96, 1)),
        ],
        axis=1,
    )
    stacked = jnp.concatenate([act[:, :256], level, act[:, 128:]], axis=0)
    xh, xl = halves(stacked)
    prod[...] = product(wh[...], wl[...], xh, xl)
    following, same = [], []
    for p in range(2):
        lanes = slice(p * 128, p * 128 + 128)
        first, second, third = [
            columns_joined(
                *(prod[(3 * a + j) * OUT : (3 * a + j + 1) * OUT, lanes] for j in range(3))
            )
            for a in range(3)
        ]
        own, moved = frames_moved(second)
        same.append(third + own)
        following.append(first + moved)
    next_mine[...] = one_frame(*following, c == 1)
    next_other[...] = one_frame(*following, c == 0)
    own_mine[...] = one_frame(*same, c == 1)
    own_other[...] = one_frame(*same, c == 0)


def norm_kernel(at, *refs):
    pieces, (strip, gain) = refs[:4], refs[4:6]
    blocked_out, normed_out, total = refs[6:]
    for k in range(CHIPS):
        chip = chip_away(at, -k)
        start = pl.multiple_of(chip * (2 * OUT), 8)
        total[pl.ds(start, 2 * OUT), :] = pieces[k][...]
    frame = total[...] + strip[...]
    blocked_out[...] = frame
    mean = jnp.mean(frame * frame, axis=0, keepdims=True)
    normed_out[...] = frame * lax.rsqrt(mean + 1e-6) * gain[...]


def query_kernel(at, blocked, normed, w_score, queries_out, rest_out, cells):
    y = at[2]
    cells[...] = blocked[...].T
    for r in range(4):
        start = pl.multiple_of(32 * r + 8 * y, 8)
        rest_out[8 * r : 8 * r + 8, :] = cells[pl.ds(start, 8), :]
    queries_out[...] = jnp.dot(
        normed[...].T, w_score[...], precision=lax.Precision.HIGHEST, preferred_element_type=F32
    )


def mix_kernel(at, queries, keys_a, keys_b, *refs):
    outs, state = refs[:CHIPS], refs[CHIPS]
    q = queries[...]
    scores = [
        jnp.dot(q, k[...], precision=lax.Precision.HIGHEST, preferred_element_type=F32)
        for k in (keys_a, keys_b)
    ]
    top = jnp.max(jnp.maximum(*scores), axis=1, keepdims=True)
    weights = [jnp.exp(s - top) for s in scores]
    denom = jnp.sum(weights[0] + weights[1], axis=1, keepdims=True)
    state[:, :C] = dot(
        jnp.concatenate([thrice(p, 1, left=True) for p in weights], axis=1),
        jnp.concatenate([thrice(k[...], 1) for k in (keys_a, keys_b)], axis=1),
        depth=1,
    )
    state[:, C:] = jnp.where(lane_of((128, 128)) < 64, top, denom)
    for k in range(CHIPS):
        chip = chip_away(at, k)
        for r in range(4):
            start = pl.multiple_of(32 * r + 8 * chip, 8)
            outs[k][8 * r : 8 * r + 8, :] = state[pl.ds(start, 8), :]


def merged(states):
    tops = [x[:, C : C + 1] for x in states]
    top = jnp.maximum(jnp.maximum(tops[0], tops[1]), jnp.maximum(tops[2], tops[3]))
    factors = [jnp.exp(t - top) for t in tops]
    denom = sum(f * x[:, C + 64 : C + 65] for f, x in zip(factors, states))
    return sum(f * x[:, :C] for f, x in zip(factors, states)) / denom


def project_kernel(at, a, b, c, d, w_mixed, bias, rest, mine_out, other_out):
    mixed = merged([x[...] for x in (a, b, c, d)])
    projected = dot(thrice(mixed, 1, left=True), thrice(w_mixed[...], 0))
    done = rest[...] + (projected + bias[...])
    done = done.reshape(4, 8, C)
    left, right = done[:, :4], done[:, 4:]
    mine_out[...] = jnp.where(at[3] == 0, left, right)
    other_out[...] = jnp.where(at[3] == 0, right, left)


def split_weights(kernel, order):
    w = jnp.transpose(kernel, order)
    w = w.reshape(-1, math.prod(w.shape[order.index(0) + 1 :]))
    high = lax.reduce_precision(w, 8, 7)
    return high.astype(BF16), (w - high).astype(BF16)


def per_device(
    latents,
    first_gain,
    first_kernel,
    first_bias,
    second_gain,
    second_kernel,
    second_bias,
    attn_gain,
    w_query,
    w_key,
    w_value,
    w_out,
    out_bias,
):
    wa = lax.axis_index("wa")
    at = jnp.stack([lax.axis_index("ta"), lax.axis_index("ha"), wa // 2, wa % 2]).astype(jnp.int32)
    column = lambda v: v.reshape(C, 1)

    first_w = split_weights(first_kernel[:, :2], (1, 2, 3, 0, 4))
    first_w_own = split_weights(first_kernel[:, 2:], (1, 2, 3, 0, 4))
    second_w = split_weights(second_kernel, (1, 3, 0, 2, 4))
    w_score = lax.dot_general(
        w_query,
        w_key,
        (((1,), (1,)), ((), ())),
        precision=lax.Precision.HIGHEST,
        preferred_element_type=F32,
    ) * (1.0 / math.sqrt(C))
    w_mixed = jnp.dot(w_value, w_out, precision=lax.Precision.HIGHEST, preferred_element_type=F32)

    operand = lambda *shape: jax.ShapeDtypeStruct(shape, BF16)
    following, earlier, strip, *x = call(
        first_conv_kernel,
        [(OUT, 384), (OUT, 384), (C, 256), operand(C, 256), operand(C, 256)],
        *gathered(latents),
        column(first_gain),
        *first_w,
        scratch=[pltpu.VMEM((256, C), F32), pltpu.VMEM((18 * OUT, 256), F32)],
        scalars=at,
        flops=1_000_000_000,
    )
    arrived = shifted(following, "ta", 1)
    own, strip = call(
        first_conv_own_kernel,
        [(OUT, 384), (C, 128)],
        *x,
        *first_w_own,
        earlier,
        strip,
        scratch=[pltpu.VMEM((9 * OUT, 256), F32)],
        scalars=at,
        flops=500_000_000,
    )
    own = own + jnp.where(at[0] > 0, arrived, 0.0)
    top, mid, bottom = own[:, :128], own[:, 128:256], own[:, 256:]
    above, below = shifted(bottom, "ha", 1), shifted(top, "ha", -1)
    second_row = (lax.broadcasted_iota(jnp.int32, (1, 128), 1) & 63) >= 32
    b = lax.dynamic_slice_in_dim(column(first_bias), wa * OUT, OUT)
    inside = jnp.where(at[1] > 0, True, second_row)
    top = jnp.where(inside, top + b + jnp.where(at[1] > 0, above, 0.0), 0.0)
    inside = jnp.where(at[1] < 7, True, ~second_row)
    bottom = jnp.where(inside, bottom + b + jnp.where(at[1] < 7, below, 0.0), 0.0)
    inner = jnp.concatenate([top, mid + b, bottom], axis=1)
    next_mine, next_other, mine, other = call(
        second_conv_kernel,
        [(OUT, 128)] * 4,
        *gathered(inner),
        column(second_gain),
        *second_w,
        scratch=[pltpu.VMEM((C, 384), F32), pltpu.VMEM((9 * OUT, 256), F32)],
        scalars=at,
        flops=1_000_000_000,
    )
    arrived = shifted(next_mine, "ta", 1)
    n = 2 * CHIPS
    arrived_other = lax.ppermute(
        next_other,
        ("ta", "wa"),
        [(t * n + i, (t + 1) % 4 * n + (i ^ 1)) for t in range(4) for i in range(n)],
    )
    mine = mine + jnp.where(at[0] > 0, arrived, 0.0)
    other = sibling(other) + jnp.where(at[0] > 0, arrived_other, 0.0)
    even = wa % 2 == 0
    change = jnp.concatenate(
        [jnp.where(even, mine, other), jnp.where(even, other, mine)], axis=0
    ) + lax.dynamic_slice_in_dim(column(second_bias), at[2] * (2 * OUT), 2 * OUT)
    blocked, normed = call(
        norm_kernel,
        [(C, 128), (C, 128)],
        change,
        *across_chips([change] * (CHIPS - 1)),
        strip,
        column(attn_gain),
        scratch=[pltpu.VMEM((C, 128), F32)],
        scalars=at,
    )
    keys = []
    for n in range(2):
        pairs = []
        for h in range(8):
            for w in range(8):
                offset = Z_OFFSETS[w // 2][n] * (1 if w % 2 == 0 else -1)
                pairs.append((((h + offset) % 8) * 8 + w, h * 8 + w))
        keys.append(lax.ppermute(normed, ("ha", "wa"), pairs))
    queries, rest = call(
        query_kernel,
        [(128, C), (32, C)],
        blocked,
        normed,
        w_score,
        scratch=[pltpu.VMEM((128, C), F32)],
        scalars=at,
    )
    states = call(
        mix_kernel,
        [(32, C + 128)] * CHIPS,
        queries,
        *keys,
        scratch=[pltpu.VMEM((128, C + 128), F32)],
        scalars=at,
    )
    mine, other = call(
        project_kernel,
        [(4, 4, C), (4, 4, C)],
        states[0],
        *across_chips(states[1:]),
        w_mixed,
        out_bias.reshape(1, C),
        rest,
        scalars=at,
    )
    other = sibling(other)
    return jnp.stack([jnp.where(even, mine, other), jnp.where(even, other, mine)])


def solution(mesh):
    in_specs = (
        P("ta", "ha", "wa", None),
        P(),
        P("wa", None, None, None, None),
        P(),
        P(),
        P("wa", None, None, None, None),
        P(),
        P(),
        P(),
        P(),
        P(),
        P(),
        P(),
    )
    out_specs = P("ta", "ha", "wa", None)
    return jax.shard_map(
        per_device, mesh=mesh, in_specs=in_specs, out_specs=out_specs, check_vma=False
    )
```
